32 devices in a mesh: table: 16 (over z, y, x), expert: 2 (over core).
Axes of the slice: x: 2, y: 2, z: 4, core: 2. Of those that a mesh axis runs over, the one named last changes fastest.
Arguments:
- table: bfloat16 [16, 512, 256], P('table'), may hold values from -127 to 127, as said below
- row_scale: float32 [16, 512], P('table'), may hold values from 0.3 to 3
- windows: int32 [16, 2, 256], P('table', 'expert'), may hold values from 0 to 511, as said below
- bag_idx: int32 [16, 2, 2048, 8], P('table', 'expert'), may hold values from 0 to 255
- bag_len: int32 [16, 2, 2048], P('table', 'expert'), may hold values from 1 to 8
- feat_gain: float32 [16, 256], replicated, may hold values from 0.03 to 0.3
- norm_gain: float32 [256], replicated, may hold values from 0.5 to 1.5
- expert_ids: int32 [2, 2048, 1], P('expert', 'table'), may hold values from 0 to 15; in each aligned block of 128 rows (0 to 127, 128 to 255, ..., all dimensions but the last counted through in order) at most 16 rows name the same one
- w_in: bfloat16 [16, 256, 4096], P('table', None, 'expert'), may hold values from -0.375 to 0.375
- w_out: bfloat16 [16, 4096, 256], P('table', 'expert'), may hold values from -0.09375 to 0.09375
- w_tow1: bfloat16 [3, 256, 256], replicated, may hold values from -0.375 to 0.375
- w_tow2: float32 [3, 256], replicated, may hold values from -1.5 to 1.5
- targets: float32 [2, 2048, 3], P('expert', 'table'), may hold values from 0 to 1
Outputs:
- predictions: float32 [2, 2048, 3], P('expert', 'table')
- grad_table: float32 [16, 512, 256], P('table', 'expert')
- grad_w_in: float32 [16, 256, 4096], P('table', None, 'expert')
- grad_w_out: float32 [16, 4096, 256], P('table', 'expert')
The draws below stay inside these ranges and needn't reach their ends.
Inputs may be any that keep to these rules, and one draw needn't show every extreme that they name: `table`: every entry is an integer. Each row windows[f, g] holds 256 distinct row numbers of feature f's table. `expert_ids`: in each aligned block of 128 samples (the samples of one device) no expert is named by more than 16 samples.
All inputs are finite; a program needn't handle non-finite values.
Results may differ from the reference program's by a relative error of at most 0.02.
Values may be sent and summed in bfloat16 or wider, within the bound.
A program may use at most 128 MiB of HBM per device.

```python
import math
import jax
import jax.numpy as jnp
import numpy as np
from jax import lax

E = 256
FF = 4096
TH = 256
L = 8
WIN = 256
B_DEV = 128
TROWS = 512
F = 16
EXPERTS = 16
GROUPS = 2
B_GROUP = 2048
CAP = 16
N_EXPERT = 2


def draw_table(key, part):
    codes = jax.random.randint(jax.random.fold_in(key, 29), (F, TROWS, E), -127, 128)
    return codes.astype(jnp.float32).astype(jnp.bfloat16)


def draw_windows(key, part):
    keys = jax.random.split(jax.random.fold_in(key, 17), F * GROUPS)

    def one_window(subkey):
        return jax.random.permutation(subkey, TROWS)[:WIN]
    return jax.vmap(one_window)(keys).reshape(F, GROUPS, WIN).astype(jnp.int32)


def touch_ends(values, stream_key, least, largest):
    dims = values.shape
    spot = [jax.random.randint(jax.random.fold_in(stream_key, axis), (), 0, dims[axis]) for axis in range(len(dims))]
    values = values.at[tuple(spot)].set(least)
    longest = dims.index(max(dims))
    spot[longest] = (spot[longest] + 1) % dims[longest]
    return values.at[tuple(spot)].set(largest)


def block_levels(key, dims, cuts, low, largest):
    gain, own = 1.0, jax.random.fold_in(key, 6)
    for dim, blocks in cuts:
        heights = jnp.exp(jax.random.uniform(jax.random.fold_in(own, dim), (blocks,), jnp.float32, low / len(cuts), largest / len(cuts)))
        gain = gain * jnp.repeat(heights, dims[dim] // blocks).reshape([-1 if axis == dim else 1 for axis in range(len(dims))])
    return gain


def cumulative_ranks(count, lean):
    weights = [(1 << 20) // math.isqrt(grade ** lean) + 1 for grade in range(1, count + 1)]
    scale = 1 + sum(weights) // (1 << 30)
    return np.cumsum(np.array([max(1, weight // scale) for weight in weights]))


def ranked(own_key, dims, amount, slope):
    table = cumulative_ranks(amount, slope)
    ticket = jax.random.randint(jax.random.fold_in(own_key, 1), dims, 0, int(table[amount - 1]))
    grade = jnp.searchsorted(jnp.asarray(table, jnp.int32), ticket, side="right")
    return jax.random.permutation(jax.random.fold_in(own_key, 2), amount)[grade].astype(jnp.int32)


def shared_out(key, own, number, rows, amount, top, limit, slope):
    sequence = jax.random.permutation(key, amount)
    heavy_load, usual = shares(amount, rows * top, limit, slope, True), shares(amount, rows * top, limit, slope, False)
    places = jnp.arange(amount)

    def named(sizes, offset_by):
        used = int((sizes > 0).sum())
        fixed = max(1, used // 4)
        shifted = fixed + (places - fixed + offset_by * (used - fixed)) % max(1, amount - fixed)
        return jnp.zeros((amount,), jnp.int32).at[sequence[jnp.where(places < fixed, places, shifted)]].set(jnp.asarray(sizes, jnp.int32))

    sizes = jnp.where(number % 4 == 0, named(heavy_load, number // 4), named(usual, number - number // 4 - 1))
    mixed = jax.random.permutation(jax.random.fold_in(own, 3), amount)
    donor, taker = mixed[0:amount // 2 * 2:2], mixed[1:amount // 2 * 2:2]
    slack = jnp.minimum(sizes[donor] - 1, limit - sizes[taker]) // 2
    slack = jnp.where((donor == sequence[0]) | (taker == sequence[0]) | (sizes[taker] == 0), 0, jnp.maximum(slack, 0))
    shifted = jax.random.randint(jax.random.fold_in(own, 4), (amount // 2,), 0, 1 << 20) % (slack + 1)
    sizes = sizes.at[donor].add(-shifted).at[taker].add(shifted)
    labels = jnp.searchsorted(jnp.cumsum(sizes), jnp.arange(rows * top), side="right").astype(jnp.int32)
    grid = labels.reshape(top, rows).T
    grid = grid[jax.random.permutation(jax.random.fold_in(own, 1), rows)]
    offset_by = jax.random.randint(jax.random.fold_in(own, 2), (rows, 1), 0, top)
    return jnp.take_along_axis(grid, (jnp.arange(top)[None, :] + offset_by) % top, axis=1)


def shares(amount, total, reach, skew, full):
    portions = [(1 << 20) // math.isqrt(standing ** skew) + 1 for standing in range(1, amount + 1)]
    largest = reach if full else min(reach, max(-(-total // amount), total * portions[0] // sum(portions)))
    least = 1 if total - largest >= amount - 1 else 0
    counts, surplus = [largest] + [least] * (amount - 1), total - largest - least * (amount - 1)
    while surplus > 0:
        candidates = [i for i in range(1, amount) if counts[i] < largest] or [i for i in range(1, amount) if counts[i] < reach]
        pool, left = sum([portions[i] for i in candidates]), surplus
        for i in candidates:
            more = min(reach - counts[i], max(1, left * portions[i] // pool), surplus)
            counts[i] = counts[i] + more
            surplus = surplus - more
    return np.array(counts)


def scatter_about(stream_key, extent, scale, limit, cuts=(), kind=jnp.bfloat16):
    values = jax.random.normal(stream_key, extent, jnp.float32) * scale
    if len(cuts) > 0:
        values = block_levels(stream_key, extent, cuts, -0.22, 0.18) * values
    return jnp.clip(values, min=-limit, max=limit).astype(kind)


def setup_inputs(seed: int = 0) -> dict:
    streams_of = jax.random.split(jax.random.key(seed), 14)
    table = draw_table(jax.random.fold_in(streams_of[13], 71), 0)
    row_scale = jnp.clip(jnp.exp(math.log(3.0) - 2.3025851 * jax.random.uniform(streams_of[1], (F, TROWS), jnp.float32) ** block_levels(streams_of[1], (F, TROWS), ((0, 16),), -0.2, 0.2)), 0.3, 3.0)
    windows = draw_windows(jax.random.fold_in(streams_of[13], 71), 0)
    bag_idx = touch_ends(ranked(streams_of[3], (F, GROUPS, B_GROUP, L), WIN, 1), jax.random.fold_in(streams_of[3], 3), 0, WIN - 1).astype(jnp.int32)
    bag_len = touch_ends(jax.random.randint(streams_of[4], (F, GROUPS, B_GROUP), 1, L + 1), jax.random.fold_in(streams_of[4], 1), 1, L).astype(jnp.int32)
    feat_gain = jnp.clip(jnp.exp(jax.random.uniform(streams_of[5], (F, E), jnp.float32, math.log(0.03), math.log(0.3))), 0.03, 0.3)
    norm_gain = jnp.clip(1.0 + 0.1 * jax.random.normal(streams_of[6], (E,), jnp.float32), 0.5, 1.5)
    expert_ids_keys = jax.random.split(jax.random.fold_in(streams_of[7], 1), GROUPS * B_GROUP // B_DEV)
    expert_ids_turns = jax.random.permutation(jax.random.fold_in(streams_of[7], 3), GROUPS * B_GROUP // B_DEV)
    expert_ids = jax.vmap(lambda own, number: shared_out(jax.random.fold_in(streams_of[7], 2), own, number, B_DEV, EXPERTS, 1, CAP, 2))(expert_ids_keys, expert_ids_turns).reshape((GROUPS, B_GROUP, 1))
    w_in = scatter_about(streams_of[8], (EXPERTS, E, FF), E ** -0.5, 0.375, ((0, 16), (2, 2)))
    w_out = scatter_about(streams_of[9], (EXPERTS, FF, E), FF ** -0.5, 0.09375, ((0, 16), (1, 2)))
    w_tow1 = scatter_about(streams_of[10], (3, E, TH), E ** -0.5, 0.375)
    w_tow2 = scatter_about(streams_of[11], (3, TH), 0.25, 1.5, (), jnp.float32)
    targets = jnp.clip(1.0 * jax.random.uniform(streams_of[12], (GROUPS, B_GROUP, 3), jnp.float32) ** block_levels(streams_of[12], (GROUPS, B_GROUP, 3), ((0, 2), (1, 16)), -0.2, 0.2), 0.0, 1.0)
    return dict(table=table, row_scale=row_scale, windows=windows, bag_idx=bag_idx, bag_len=bag_len, feat_gain=feat_gain, norm_gain=norm_gain, expert_ids=expert_ids, w_in=w_in, w_out=w_out, w_tow1=w_tow1, w_tow2=w_tow2, targets=targets)


code_range = 127.0

def silu_slope(values):
    sigma = jax.nn.sigmoid(values)
    return sigma * (1.0 + values * (1.0 - sigma))

def rounded(values):
    return lax.optimization_barrier(values.astype(jnp.bfloat16)).astype(jnp.float32)

def column_partials(left, right):
    shard = FF // N_EXPERT
    left_split = left.astype(jnp.float32).reshape(left.shape[0], N_EXPERT, shard)
    right_split = right.astype(jnp.float32).reshape(N_EXPERT, shard, right.shape[-1])
    partials = jnp.einsum('rkf,kfe->kre', left_split, right_split)
    return lax.optimization_barrier(jnp.sum(rounded(partials), axis=0))

def reference(table, row_scale, windows, bag_idx, bag_len, feat_gain, norm_gain, expert_ids, w_in, w_out, w_tow1, w_tow2, targets):
    feature_ids = jnp.arange(F, dtype=jnp.int32)
    group_ids = jnp.arange(GROUPS, dtype=jnp.int32)
    picked = table[feature_ids[:, None, None], windows].astype(jnp.float32)
    scales = row_scale[feature_ids[:, None, None], windows]
    dequant = (picked * scales[..., None] / code_range).astype(jnp.bfloat16)
    slots = jnp.arange(L, dtype=jnp.int32)

    def live_mask(lengths):
        return (slots[None, :] < lengths[:, None]).astype(jnp.float32)

    def group_sum(group):

        def feature_step(carry, feature):
            rows = jnp.take(dequant[feature, group], bag_idx[feature, group], axis=0).astype(jnp.float32)
            pooled = lax.optimization_barrier(jnp.sum(rows * live_mask(bag_len[feature, group])[:, :, None], axis=1)).astype(jnp.bfloat16)
            return (carry + pooled.astype(jnp.float32) * feat_gain[feature], None)
        result, _ = lax.scan(feature_step, jnp.zeros((B_GROUP, E), jnp.float32), feature_ids)
        return result
    summed = lax.map(group_sum, group_ids).reshape(GROUPS * B_GROUP, E)
    inverse = lax.rsqrt(lax.optimization_barrier(jnp.mean(summed * summed, axis=-1, keepdims=True)) + 1e-05)
    normed = (summed * inverse * norm_gain).astype(jnp.bfloat16)
    blocks = GROUPS * B_GROUP // B_DEV
    chosen = expert_ids.reshape(blocks, B_DEV)
    member = (chosen[:, :, None] == jnp.arange(EXPERTS, dtype=jnp.int32)[None, None, :]).astype(jnp.int32)
    ranks = jnp.cumsum(member, axis=1) - member
    slot_of = lax.optimization_barrier(jnp.sum(ranks * member, axis=-1))
    block_ids = jnp.arange(blocks, dtype=jnp.int32)[:, None]
    per_expert = blocks * CAP
    position = (chosen * per_expert + block_ids * CAP + slot_of).reshape(-1).astype(jnp.int32)

    def to_experts(values):
        buffer = jnp.zeros((EXPERTS * per_expert, E), values.dtype).at[position].set(values)
        return buffer.reshape(EXPERTS, per_expert, E)

    def expert_forward(operands):
        rows, weight_in, weight_out = operands
        pre_act = jnp.dot(rows, weight_in, preferred_element_type=jnp.float32)
        hidden = jax.nn.silu(pre_act).astype(jnp.bfloat16)
        return column_partials(hidden, weight_out).astype(jnp.bfloat16)
    routed = to_experts(normed)
    expert_out = lax.map(expert_forward, (routed, w_in, w_out)).reshape(EXPERTS * per_expert, E)
    mixture = expert_out[position].astype(jnp.float32)
    joined = (normed.astype(jnp.float32) + mixture).astype(jnp.bfloat16)
    tower_pre = jnp.einsum('be,kem->kbm', joined.astype(jnp.float32), w_tow1.astype(jnp.float32))
    logits = lax.optimization_barrier(jnp.sum(jax.nn.silu(tower_pre) * w_tow2[:, None, :], axis=-1))
    predicted = jnp.stack([jax.nn.sigmoid(logits[0]), jax.nn.sigmoid(logits[1]), logits[2]], axis=-1)
    logit_grad = predicted - targets.reshape(-1, 3)
    tower_grad = (logit_grad.T[:, :, None] * w_tow2[:, None, :] * silu_slope(tower_pre)).astype(jnp.bfloat16)
    joined_grad = jnp.einsum('kbm,kem->be', tower_grad.astype(jnp.float32), w_tow1.astype(jnp.float32)).astype(jnp.bfloat16)

    def expert_backward(operands):
        rows, grads, weight_in, weight_out = operands
        pre_act = jnp.dot(rows, weight_in, preferred_element_type=jnp.float32)
        hidden = jax.nn.silu(pre_act).astype(jnp.bfloat16)
        grad_hidden = jnp.dot(grads, weight_out.T, preferred_element_type=jnp.float32)
        grad_pre = (grad_hidden * silu_slope(pre_act)).astype(jnp.bfloat16)
        grad_out = jnp.dot(hidden.T, grads, preferred_element_type=jnp.float32)
        grad_in = jnp.dot(rows.T, grad_pre, preferred_element_type=jnp.float32)
        input_grad = column_partials(grad_pre, weight_in.T).astype(jnp.bfloat16)
        return (grad_in, grad_out, input_grad)
    grad_w_in, grad_w_out, input_grad = lax.map(expert_backward, (routed, to_experts(joined_grad), w_in, w_out))
    mixture_grad = input_grad.reshape(EXPERTS * per_expert, E)[position].astype(jnp.float32)
    normed_grad = joined_grad.astype(jnp.float32) + mixture_grad
    scaled_grad = normed_grad * norm_gain
    summed_grad = inverse * (scaled_grad - summed * inverse * inverse * lax.optimization_barrier(jnp.mean(scaled_grad * summed, axis=-1, keepdims=True)))
    summed_grad = summed_grad.reshape(GROUPS, B_GROUP, E)

    def group_grad(group):
        group_values = summed_grad[group]

        def feature_grad(feature):
            pooled_grad = rounded(group_values * feat_gain[feature])
            terms = pooled_grad[:, None, :] * live_mask(bag_len[feature, group])[:, :, None]
            return jnp.zeros((WIN, E), jnp.float32).at[bag_idx[feature, group].reshape(-1)].add(terms.reshape(-1, E))
        return lax.map(feature_grad, feature_ids)
    window_grad = jnp.swapaxes(lax.map(group_grad, group_ids), 0, 1)

    def table_rows(operands):
        rows_grad, row_ids = operands
        return jnp.zeros((TROWS, E), jnp.float32).at[row_ids.reshape(-1)].add(rows_grad.reshape(-1, E))
    grad_table = lax.map(table_rows, (window_grad, windows))
    return (predicted.reshape(GROUPS, B_GROUP, 3), grad_table, grad_w_in, grad_w_out)
```

```python
import functools

import jax
import jax.numpy as jnp
from jax import lax
from jax.experimental import pallas as pl
from jax.experimental.pallas import tpu as pltpu
from jax.sharding import PartitionSpec as P

code_range = 127.0


def silu_slope(values):
    sigma = jax.nn.sigmoid(values)
    return sigma * (1.0 + values * (1.0 - sigma))


def bag_counts(indices, lengths, window):
    slots = jnp.arange(indices.shape[1], dtype=jnp.int32)
    live = jnp.where(slots[:, None] < lengths[None, :], indices.T, -1)
    positions = jnp.arange(window, dtype=jnp.int32)
    hits = (live[:, None, :] == positions[None, :, None]).astype(jnp.float32)
    return jnp.sum(hits, axis=0).astype(jnp.bfloat16)


def exchange_kernel(owners, columns, shared, x_ref, o_ref, send_sem, recv_sem, own_sem):
    devices = owners * columns
    mine = lax.axis_index("expert") * owners + lax.axis_index("table")
    barrier = pltpu.get_barrier_semaphore()

    def place(step):
        other = lax.rem(mine + step, devices)
        return other, lax.rem(other, owners), lax.div(other, owners)

    def greet(step, carry):
        _, row, column = place(step)
        pl.semaphore_signal(
            barrier, inc=1, device_id=(row, column), device_id_type=pl.DeviceIdType.MESH
        )
        return carry

    def copy(step):
        other, row, column = place(step)
        return pltpu.make_async_remote_copy(
            src_ref=x_ref.at[row if shared else other],
            dst_ref=o_ref.at[mine],
            send_sem=send_sem.at[step],
            recv_sem=recv_sem.at[step],
            device_id=(row, column),
            device_id_type=pl.DeviceIdType.MESH,
        )

    def send(step, carry):
        copy(step).start()
        return carry

    def settle(step, carry):
        copy(step).wait()
        return carry

    lax.fori_loop(1, devices, greet, 0)
    own = pltpu.make_async_copy(
        x_ref.at[lax.axis_index("table") if shared else mine], o_ref.at[mine], own_sem
    )
    own.start()
    pl.semaphore_wait(barrier, devices - 1)
    lax.fori_loop(1, devices, send, 0)
    own.wait()
    lax.fori_loop(1, devices, settle, 0)


def exchange(blocks, shared, collective_id):
    owners, columns = lax.axis_size("table"), lax.axis_size("expert")
    devices = owners * columns
    return pl.pallas_call(
        functools.partial(exchange_kernel, owners, columns, shared),
        out_shape=jax.ShapeDtypeStruct((devices,) + blocks.shape[1:], blocks.dtype),
        in_specs=[pl.BlockSpec(memory_space=pltpu.VMEM)],
        out_specs=pl.BlockSpec(memory_space=pltpu.VMEM),
        scratch_shapes=[
            pltpu.SemaphoreType.DMA((devices,)),
            pltpu.SemaphoreType.DMA((devices,)),
            pltpu.SemaphoreType.DMA,
        ],
        compiler_params=pltpu.CompilerParams(collective_id=collective_id, has_side_effects=True),
    )(blocks)


def direct():
    return lax.axis_size("expert") == 2


def dispatch(buffer, collective_id):
    if direct():
        return exchange(buffer, True, collective_id).reshape(-1, buffer.shape[-1])
    arrived = lax.all_to_all(buffer, "table", split_axis=0, concat_axis=0, tiled=True)
    columns = lax.all_gather(arrived[None], "expert", axis=0, tiled=True)
    return columns.reshape(-1, buffer.shape[-1])


def send_back(partial, experts, capacity, collective_id):
    width = partial.shape[-1]
    partial = partial.astype(jnp.bfloat16)
    if direct():
        arrived = exchange(partial.reshape(-1, capacity, width), False, collective_id)
        arrived = arrived.reshape(2, experts * capacity, width).astype(jnp.float32)
        return (arrived[0] + arrived[1]).astype(jnp.bfloat16)
    summed = lax.psum_scatter(partial, "expert", scatter_dimension=0, tiled=True)
    arrived = lax.all_to_all(
        summed.reshape(experts, capacity, width), "table", split_axis=0, concat_axis=0, tiled=True
    )
    return arrived.reshape(experts * capacity, width)


def sum_rows(row_grad):
    row_grad = row_grad.astype(jnp.bfloat16)
    if direct():
        half = row_grad.shape[0] // 2
        column = lax.axis_index("expert")
        theirs = lax.dynamic_slice_in_dim(row_grad, (1 - column) * half, half, 0)
        ours = lax.dynamic_slice_in_dim(row_grad, column * half, half, 0)
        arrived = lax.ppermute(theirs, "expert", [(0, 1), (1, 0)])
        return ours.astype(jnp.float32) + arrived.astype(jnp.float32)
    return lax.psum_scatter(row_grad, "expert", scatter_dimension=0, tiled=True).astype(jnp.float32)


def local(
    table,
    row_scale,
    windows,
    bag_idx,
    bag_len,
    feat_gain,
    norm_gain,
    expert_ids,
    w_in,
    w_out,
    w_tow1,
    w_tow2,
    targets,
):
    owners = lax.axis_size("table")
    samples = expert_ids.shape[1]
    capacity = max(2, 2 * samples // owners)
    local_rows = owners * capacity
    contract_rows = (((0,), (0,)), ((), ()))
    contract_cols = (((1,), (1,)), ((), ()))
    window = windows[0, 0]
    row_select = (
        jnp.arange(table.shape[1], dtype=jnp.int32)[:, None] == window[None, :]
    ).astype(jnp.bfloat16)
    rows = (table[0].astype(jnp.float32) * row_scale[0][:, None] / code_range).astype(jnp.bfloat16)
    dequant = lax.dot_general(
        row_select, rows, contract_rows, preferred_element_type=jnp.float32
    ).astype(jnp.bfloat16)
    counts = bag_counts(bag_idx[0, 0], bag_len[0, 0], window.shape[0])
    pooled = lax.dot_general(counts, dequant, contract_rows, preferred_element_type=jnp.float32)
    own_gain = lax.dynamic_slice_in_dim(feat_gain, lax.axis_index("table"), 1, 0)
    weighted = (pooled.astype(jnp.bfloat16).astype(jnp.float32) * own_gain).astype(jnp.bfloat16)
    summed = lax.psum_scatter(weighted, "table", scatter_dimension=0, tiled=True).astype(
        jnp.float32
    )
    inverse = lax.rsqrt(jnp.mean(summed * summed, axis=-1, keepdims=True) + 1e-05)
    normed = (summed * inverse * norm_gain).astype(jnp.bfloat16)
    chosen = expert_ids[0, :, 0]
    member = (chosen[:, None] == jnp.arange(owners, dtype=jnp.int32)[None, :]).astype(jnp.bfloat16)
    order = jnp.arange(samples, dtype=jnp.int32)
    earlier = (order[None, :] < order[:, None]).astype(jnp.bfloat16)
    ranks = jnp.dot(earlier, member, preferred_element_type=jnp.float32)
    slot_of = jnp.sum(ranks * member.astype(jnp.float32), axis=1).astype(jnp.int32)
    target_slot = chosen * capacity + slot_of
    placing = (jnp.arange(local_rows, dtype=jnp.int32)[:, None] == target_slot[None, :]).astype(
        jnp.bfloat16
    )
    outgoing = jnp.dot(placing, normed, preferred_element_type=jnp.float32).astype(jnp.bfloat16)
    gathered = dispatch(outgoing.reshape(owners, capacity, outgoing.shape[-1]), 1)
    weight_in = w_in[0]
    weight_out = w_out[0]
    pre_act = jnp.dot(gathered, weight_in, preferred_element_type=jnp.float32)
    hidden = jax.nn.silu(pre_act).astype(jnp.bfloat16)

    forward = jnp.dot(hidden, weight_out, preferred_element_type=jnp.float32)
    expert_out = send_back(forward, owners, capacity, 2)
    mixture = lax.dot_general(
        placing, expert_out, contract_rows, preferred_element_type=jnp.float32
    )
    joined = (normed.astype(jnp.float32) + mixture).astype(jnp.bfloat16)
    tower_pre = jnp.einsum("be,kem->kbm", joined, w_tow1, preferred_element_type=jnp.float32)
    logits = jnp.sum(jax.nn.silu(tower_pre) * w_tow2[:, None, :], axis=-1)
    predicted = jnp.stack(
        [jax.nn.sigmoid(logits[0]), jax.nn.sigmoid(logits[1]), logits[2]], axis=-1
    )
    logit_grad = predicted - targets[0]
    tower_grad = (logit_grad.T[:, :, None] * w_tow2[:, None, :] * silu_slope(tower_pre)).astype(
        jnp.bfloat16
    )
    joined_grad = jnp.einsum(
        "kbm,kem->be", tower_grad, w_tow1, preferred_element_type=jnp.float32
    ).astype(jnp.bfloat16)
    back_rows = jnp.dot(placing, joined_grad, preferred_element_type=jnp.float32).astype(
        jnp.bfloat16
    )
    gathered_grad = dispatch(back_rows.reshape(owners, capacity, back_rows.shape[-1]), 3)
    grad_hidden = lax.dot_general(
        gathered_grad, weight_out, contract_cols, preferred_element_type=jnp.float32
    )
    grad_pre = (grad_hidden * silu_slope(pre_act)).astype(jnp.bfloat16)
    grad_out = lax.dot_general(
        hidden, gathered_grad, contract_rows, preferred_element_type=jnp.float32
    )
    grad_in = lax.dot_general(gathered, grad_pre, contract_rows, preferred_element_type=jnp.float32)

    backward = lax.dot_general(
        grad_pre, weight_in, contract_cols, preferred_element_type=jnp.float32
    )
    input_grad = send_back(backward, owners, capacity, 4)
    mixture_grad = lax.dot_general(
        placing, input_grad, contract_rows, preferred_element_type=jnp.float32
    )
    normed_grad = joined_grad.astype(jnp.float32) + mixture_grad
    scaled_grad = normed_grad * norm_gain
    summed_grad = inverse * (
        scaled_grad
        - summed * inverse * inverse * jnp.mean(scaled_grad * summed, axis=-1, keepdims=True)
    )
    returned = lax.all_gather(summed_grad.astype(jnp.bfloat16), "table", axis=0, tiled=True)
    window_grad = jnp.dot(counts, returned, preferred_element_type=jnp.float32) * own_gain
    row_grad = jnp.dot(
        row_select, window_grad.astype(jnp.bfloat16), preferred_element_type=jnp.float32
    )
    table_grad = sum_rows(row_grad)
    return (predicted[None], table_grad[None], grad_in[None], grad_out[None])


def solution(mesh):
    in_specs = (
        P("table", None, None),
        P("table", None),
        P("table", "expert", None),
        P("table", "expert", None, None),
        P("table", "expert", None),
        P(),
        P(),
        P("expert", "table", None),
        P("table", None, "expert"),
        P("table", "expert", None),
        P(),
        P(),
        P("expert", "table", None),
    )
    out_specs = (
        P("expert", "table", None),
        P("table", "expert", None),
        P("table", None, "expert"),
        P("table", "expert", None),
    )
    return jax.shard_map(local, mesh=mesh, in_specs=in_specs, out_specs=out_specs, check_vma=False)
```

```python
import functools

import jax
import jax.numpy as jnp
from jax import lax
from jax.experimental import pallas as pl
from jax.experimental.pallas import tpu as pltpu
from jax.sharding import PartitionSpec as P

code_range = 127.0


def silu_slope(values):
    sigma = jax.nn.sigmoid(values)
    return sigma * (1.0 + values * (1.0 - sigma))


def bag_counts(indices, lengths, window):
    slots = jnp.arange(indices.shape[1], dtype=jnp.int32)
    live = jnp.where(slots[:, None] < lengths[None, :], indices.T, -1)
    positions = jnp.arange(window, dtype=jnp.int32)
    hits = (live[:, None, :] == positions[None, :, None]).astype(jnp.float32)
    return jnp.sum(hits, axis=0).astype(jnp.bfloat16)


def here():
    return lax.axis_index("table"), lax.axis_index("expert")


def remote(src, dst, send_sem, recv_sem, slot, device):
    return pltpu.make_async_remote_copy(
        src_ref=src,
        dst_ref=dst,
        send_sem=send_sem.at[slot],
        recv_sem=recv_sem.at[slot],
        device_id=device,
        device_id_type=pl.DeviceIdType.MESH,
    )


def meet(peers):
    barrier = pltpu.get_barrier_semaphore()
    for peer in peers:
        pl.semaphore_signal(barrier, inc=1, device_id=peer, device_id_type=pl.DeviceIdType.MESH)
    pl.semaphore_wait(barrier, len(peers))


def dispatch_kernel(owners, x_ref, o_ref, send_sem, recv_sem, own_sem):
    row, column = here()
    sibling = (row, 1 - column)
    peers = [(lax.rem(row + step, owners), column) for step in range(1, owners)]
    own = pltpu.make_async_copy(x_ref.at[row], o_ref.at[column, row], own_sem)
    own.start()
    meet(peers + [sibling])
    copies = [
        remote(x_ref.at[peer[0]], o_ref.at[column, row], send_sem, recv_sem, i, peer)
        for i, peer in enumerate(peers)
    ]
    for copy in copies:
        copy.start()
    own.wait()
    for copy in copies:
        copy.wait_recv()
    across = remote(
        o_ref.at[column], o_ref.at[column], send_sem, recv_sem, owners - 1, sibling
    )
    across.start()
    for copy in copies:
        copy.wait_send()
    across.wait()


def return_kernel(owners, x_ref, o_ref, theirs, total, send_sem, recv_sem, own_sem):
    row, column = here()
    sibling = (row, 1 - column)
    peers = [(lax.rem(row + step, owners), column) for step in range(1, owners)]
    meet(peers + [sibling])
    across = remote(x_ref.at[1 - column], theirs, send_sem, recv_sem, owners - 1, sibling)
    across.start()
    across.wait_recv()
    total[...] = (
        x_ref[column].astype(jnp.float32) + theirs[...].astype(jnp.float32)
    ).astype(total.dtype)
    copies = [
        remote(total.at[peer[0]], o_ref.at[row], send_sem, recv_sem, i, peer)
        for i, peer in enumerate(peers)
    ]
    for copy in copies:
        copy.start()
    own = pltpu.make_async_copy(total.at[row], o_ref.at[row], own_sem)
    own.start()
    across.wait_send()
    own.wait()
    for copy in copies:
        copy.wait()


def plane_of(row):
    layer, y, x = lax.div(row, 4), lax.rem(lax.div(row, 2), 2), lax.rem(row, 2)
    return layer, y, x


def place(layer, y, x):
    return layer * 4 + y * 2 + x


def scatter_kernel(x_ref, o_ref, diagonal, staged, arrived, up, down, send_sem, recv_sem):
    row, column = here()
    z, y, x = plane_of(row)
    beside, above = (place(z, y, 1 - x), column), (place(z, 1 - y, x), column)
    layers = [lax.rem(z + s, 4) for s in range(4)]
    meet([beside, above] + [(place(layers[s], y, x), column) for s in (1, 2, 3)])
    half = x_ref.shape[1] // 2
    first, last = pl.ds(0, half), pl.ds(half, half)
    turns = (2, 1, 3, 0)
    sent = []
    corner = {}
    for s in turns:
        target = x_ref.at[place(layers[s], 1 - y, 1 - x)]
        corner[s] = (
            remote(target.at[first], diagonal.at[s, 0], send_sem, recv_sem, s * 5, beside),
            remote(target.at[last], diagonal.at[s, 1], send_sem, recv_sem, s * 5 + 1, above),
        )
        for copy in corner[s]:
            copy.start()
            sent.append(copy)
    side = {}
    for s in turns:
        to_beside, to_above = place(layers[s], y, 1 - x), place(layers[s], 1 - y, x)
        corner[s][0].wait_recv()
        staged[s, 1, first] = (
            x_ref[to_above, first].astype(jnp.float32) + diagonal[s, 0].astype(jnp.float32)
        ).astype(staged.dtype)
        staged[s, 1, last] = x_ref[to_above, last]
        corner[s][1].wait_recv()
        staged[s, 0, first] = x_ref[to_beside, first]
        staged[s, 0, last] = (
            x_ref[to_beside, last].astype(jnp.float32) + diagonal[s, 1].astype(jnp.float32)
        ).astype(staged.dtype)
        side[s] = (
            remote(staged.at[s, 0], arrived.at[s, 0], send_sem, recv_sem, s * 5 + 2, beside),
            remote(staged.at[s, 1], arrived.at[s, 1], send_sem, recv_sem, s * 5 + 3, above),
        )
        for copy in side[s]:
            copy.start()
            sent.append(copy)
    vertical = {}
    for s in turns:
        for copy in side[s]:
            copy.wait_recv()
        partial = (
            x_ref[place(layers[s], y, x)].astype(jnp.float32)
            + arrived[s, 0].astype(jnp.float32)
            + arrived[s, 1].astype(jnp.float32)
        )
        if s == 0:
            o_ref[...] = partial
        else:
            up[s] = partial.astype(up.dtype)
            vertical[s] = remote(
                up.at[s], down.at[s], send_sem, recv_sem, s * 5 + 4, (place(layers[s], y, x), column)
            )
            vertical[s].start()
            sent.append(vertical[s])
    for s in turns[:3]:
        vertical[s].wait_recv()
        o_ref[...] += down[s].astype(jnp.float32)
    for copy in sent:
        copy.wait_send()


def gather_kernel(x_ref, o_ref, send_sem, recv_sem, own_sem):
    row, column = here()
    z, y, x = plane_of(row)
    beside, above = (place(z, y, 1 - x), column), (place(z, 1 - y, x), column)
    own = pltpu.make_async_copy(x_ref, o_ref.at[row], own_sem)
    own.start()
    meet([beside, above] + [(place(lax.rem(z + s, 4), y, x), column) for s in (1, 2, 3)])
    half = x_ref.shape[0] // 2
    first, last = pl.ds(0, half), pl.ds(half, half)
    sent = []

    def send(src, dst, slot, device):
        copy = remote(src, dst, send_sem, recv_sem, slot, device)
        copy.start()
        sent.append(copy)
        return copy

    vertical = {
        s: send(x_ref, o_ref.at[row], s * 5, (place(lax.rem(z + s, 4), y, x), column))
        for s in (1, 3, 2)
    }
    turns = (0, 1, 3, 2)
    side = {}
    for s in turns:
        mine = place(lax.rem(z + 4 - s, 4), y, x)
        source = x_ref
        if s > 0:
            vertical[s].wait_recv()
            source = o_ref.at[mine]
        side[s] = (
            send(source, o_ref.at[mine], s * 5 + 1, beside),
            send(source, o_ref.at[mine], s * 5 + 2, above),
        )
    corner = []
    for s in turns:
        layer = lax.rem(z + 4 - s, 4)
        side[s][0].wait_recv()
        block = o_ref.at[place(layer, y, 1 - x), first]
        corner.append(send(block, block, s * 5 + 3, above))
        side[s][1].wait_recv()
        block = o_ref.at[place(layer, 1 - y, x), last]
        corner.append(send(block, block, s * 5 + 4, beside))
    for copy in corner:
        copy.wait_recv()
    own.wait()
    for copy in sent:
        copy.wait_send()


def call(kernel, operand, shape, dtype, scratch, copies, collective_id):
    semaphores = [pltpu.SemaphoreType.DMA((copies,)), pltpu.SemaphoreType.DMA((copies,))]
    return pl.pallas_call(
        kernel,
        out_shape=jax.ShapeDtypeStruct(shape, dtype),
        in_specs=[pl.BlockSpec(memory_space=pltpu.VMEM)],
        out_specs=pl.BlockSpec(memory_space=pltpu.VMEM),
        scratch_shapes=[pltpu.VMEM(s, jnp.bfloat16) for s in scratch] + semaphores
        + ([] if kernel is scatter_kernel else [pltpu.SemaphoreType.DMA]),
        compiler_params=pltpu.CompilerParams(
            collective_id=collective_id, has_side_effects=True, vmem_limit_bytes=32 << 20
        ),
    )(operand)


def direct():
    return lax.axis_size("expert") == 2 and lax.axis_size("table") == 16


def dispatch(buffer, collective_id):
    if direct():
        owners = buffer.shape[0]
        kernel = functools.partial(dispatch_kernel, owners)
        arrived = call(kernel, buffer, (2,) + buffer.shape, buffer.dtype, (), owners, collective_id)
        return arrived.reshape(-1, buffer.shape[-1])
    arrived = lax.all_to_all(buffer, "table", split_axis=0, concat_axis=0, tiled=True)
    columns = lax.all_gather(arrived[None], "expert", axis=0, tiled=True)
    return columns.reshape(-1, buffer.shape[-1])


def send_back(partial, experts, capacity, collective_id):
    width = partial.shape[-1]
    partial = partial.astype(jnp.bfloat16)
    if direct():
        block = (experts, capacity, width)
        kernel = functools.partial(return_kernel, experts)
        arrived = call(
            kernel,
            partial.reshape((2,) + block),
            block,
            partial.dtype,
            (block, block),
            experts,
            collective_id,
        )
        return arrived.reshape(experts * capacity, width)
    summed = lax.psum_scatter(partial, "expert", scatter_dimension=0, tiled=True)
    arrived = lax.all_to_all(
        summed.reshape(experts, capacity, width), "table", split_axis=0, concat_axis=0, tiled=True
    )
    return arrived.reshape(experts * capacity, width)


def sum_features(weighted, samples):
    width = weighted.shape[-1]
    if direct():
        block = (samples, width)
        return call(
            scatter_kernel,
            weighted.reshape(-1, samples, width),
            block,
            jnp.float32,
            ((4, 2, samples // 2, width), (4, 2) + block, (4, 2) + block, (4,) + block, (4,) + block),
            20,
            5,
        )
    return lax.psum_scatter(weighted, "table", scatter_dimension=0, tiled=True).astype(jnp.float32)


def gather_rows(rows):
    if direct():
        owners = lax.axis_size("table")
        gathered = call(gather_kernel, rows, (owners,) + rows.shape, rows.dtype, (), 20, 6)
        return gathered.reshape(-1, rows.shape[-1])
    return lax.all_gather(rows, "table", axis=0, tiled=True)


def sum_rows(row_grad):
    row_grad = row_grad.astype(jnp.bfloat16)
    if direct():
        half = row_grad.shape[0] // 2
        column = lax.axis_index("expert")
        theirs = lax.dynamic_slice_in_dim(row_grad, (1 - column) * half, half, 0)
        ours = lax.dynamic_slice_in_dim(row_grad, column * half, half, 0)
        arrived = lax.ppermute(theirs, "expert", [(0, 1), (1, 0)])
        return ours.astype(jnp.float32) + arrived.astype(jnp.float32)
    return lax.psum_scatter(row_grad, "expert", scatter_dimension=0, tiled=True).astype(jnp.float32)


def local(
    table,
    row_scale,
    windows,
    bag_idx,
    bag_len,
    feat_gain,
    norm_gain,
    expert_ids,
    w_in,
    w_out,
    w_tow1,
    w_tow2,
    targets,
):
    owners = lax.axis_size("table")
    samples = expert_ids.shape[1]
    capacity = max(2, 2 * samples // owners)
    local_rows = owners * capacity
    contract_rows = (((0,), (0,)), ((), ()))
    contract_cols = (((1,), (1,)), ((), ()))
    window = windows[0, 0]
    row_select = (
        jnp.arange(table.shape[1], dtype=jnp.int32)[:, None] == window[None, :]
    ).astype(jnp.bfloat16)
    rows = (table[0].astype(jnp.float32) * row_scale[0][:, None] / code_range).astype(jnp.bfloat16)
    dequant = lax.dot_general(
        row_select, rows, contract_rows, preferred_element_type=jnp.float32
    ).astype(jnp.bfloat16)
    counts = bag_counts(bag_idx[0, 0], bag_len[0, 0], window.shape[0])
    pooled = lax.dot_general(counts, dequant, contract_rows, preferred_element_type=jnp.float32)
    own_gain = lax.dynamic_slice_in_dim(feat_gain, lax.axis_index("table"), 1, 0)
    weighted = (pooled.astype(jnp.bfloat16).astype(jnp.float32) * own_gain).astype(jnp.bfloat16)
    summed = sum_features(weighted, samples)
    inverse = lax.rsqrt(jnp.mean(summed * summed, axis=-1, keepdims=True) + 1e-05)
    normed = (summed * inverse * norm_gain).astype(jnp.bfloat16)
    chosen = expert_ids[0, :, 0]
    member = (chosen[:, None] == jnp.arange(owners, dtype=jnp.int32)[None, :]).astype(jnp.bfloat16)
    order = jnp.arange(samples, dtype=jnp.int32)
    earlier = (order[None, :] < order[:, None]).astype(jnp.bfloat16)
    ranks = jnp.dot(earlier, member, preferred_element_type=jnp.float32)
    slot_of = jnp.sum(ranks * member.astype(jnp.float32), axis=1).astype(jnp.int32)
    target_slot = chosen * capacity + slot_of
    placing = (jnp.arange(local_rows, dtype=jnp.int32)[:, None] == target_slot[None, :]).astype(
        jnp.bfloat16
    )
    outgoing = jnp.dot(placing, normed, preferred_element_type=jnp.float32).astype(jnp.bfloat16)
    gathered = dispatch(outgoing.reshape(owners, capacity, outgoing.shape[-1]), 1)
    weight_in = w_in[0]
    weight_out = w_out[0]
    pre_act = jnp.dot(gathered, weight_in, preferred_element_type=jnp.float32)
    hidden = jax.nn.silu(pre_act).astype(jnp.bfloat16)

    forward = jnp.dot(hidden, weight_out, preferred_element_type=jnp.float32)
    expert_out = send_back(forward, owners, capacity, 2)
    mixture = lax.dot_general(
        placing, expert_out, contract_rows, preferred_element_type=jnp.float32
    )
    joined = (normed.astype(jnp.float32) + mixture).astype(jnp.bfloat16)
    tower_pre = jnp.einsum("be,kem->kbm", joined, w_tow1, preferred_element_type=jnp.float32)
    logits = jnp.sum(jax.nn.silu(tower_pre) * w_tow2[:, None, :], axis=-1)
    predicted = jnp.stack(
        [jax.nn.sigmoid(logits[0]), jax.nn.sigmoid(logits[1]), logits[2]], axis=-1
    )
    logit_grad = predicted - targets[0]
    tower_grad = (logit_grad.T[:, :, None] * w_tow2[:, None, :] * silu_slope(tower_pre)).astype(
        jnp.bfloat16
    )
    joined_grad = jnp.einsum(
        "kbm,kem->be", tower_grad, w_tow1, preferred_element_type=jnp.float32
    ).astype(jnp.bfloat16)
    back_rows = jnp.dot(placing, joined_grad, preferred_element_type=jnp.float32).astype(
        jnp.bfloat16
    )
    gathered_grad = dispatch(back_rows.reshape(owners, capacity, back_rows.shape[-1]), 3)
    grad_hidden = lax.dot_general(
        gathered_grad, weight_out, contract_cols, preferred_element_type=jnp.float32
    )
    grad_pre = (grad_hidden * silu_slope(pre_act)).astype(jnp.bfloat16)
    grad_out = lax.dot_general(
        hidden, gathered_grad, contract_rows, preferred_element_type=jnp.float32
    )
    grad_in = lax.dot_general(gathered, grad_pre, contract_rows, preferred_element_type=jnp.float32)

    backward = lax.dot_general(
        grad_pre, weight_in, contract_cols, preferred_element_type=jnp.float32
    )
    input_grad = send_back(backward, owners, capacity, 4)
    mixture_grad = lax.dot_general(
        placing, input_grad, contract_rows, preferred_element_type=jnp.float32
    )
    normed_grad = joined_grad.astype(jnp.float32) + mixture_grad
    scaled_grad = normed_grad * norm_gain
    summed_grad = inverse * (
        scaled_grad
        - summed * inverse * inverse * jnp.mean(scaled_grad * summed, axis=-1, keepdims=True)
    )
    returned = gather_rows(summed_grad.astype(jnp.bfloat16))
    window_grad = jnp.dot(counts, returned, preferred_element_type=jnp.float32) * own_gain
    row_grad = jnp.dot(
        row_select, window_grad.astype(jnp.bfloat16), preferred_element_type=jnp.float32
    )
    table_grad = sum_rows(row_grad)
    return (predicted[None], table_grad[None], grad_in[None], grad_out[None])


def solution(mesh):
    in_specs = (
        P("table", None, None),
        P("table", None),
        P("table", "expert", None),
        P("table", "expert", None, None),
        P("table", "expert", None),
        P(),
        P(),
        P("expert", "table", None),
        P("table", None, "expert"),
        P("table", "expert", None),
        P(),
        P(),
        P("expert", "table", None),
    )
    out_specs = (
        P("expert", "table", None),
        P("table", "expert", None),
        P("table", None, "expert"),
        P("table", "expert", None),
    )
    return jax.shard_map(local, mesh=mesh, in_specs=in_specs, out_specs=out_specs, check_vma=False)
```

```python
import functools

import jax
import jax.numpy as jnp
from jax import lax
from jax.experimental import pallas as pl
from jax.experimental.pallas import tpu as pltpu
from jax.sharding import PartitionSpec as P

code_range = 127.0


def silu_slope(values):
    sigma = jax.nn.sigmoid(values)
    return sigma * (1.0 + values * (1.0 - sigma))


def bag_counts(indices, lengths, window):
    slots = jnp.arange(indices.shape[1], dtype=jnp.int32)
    live = jnp.where(slots[:, None] < lengths[None, :], indices.T, -1)
    positions = jnp.arange(window, dtype=jnp.int32)
    hits = (live[:, None, :] == positions[None, :, None]).astype(jnp.float32)
    return jnp.sum(hits, axis=0).astype(jnp.bfloat16)


def here():
    return lax.axis_index("table"), lax.axis_index("expert")


def remote(src, dst, send_sem, recv_sem, slot, device):
    return pltpu.make_async_remote_copy(
        src_ref=src,
        dst_ref=dst,
        send_sem=send_sem.at[slot],
        recv_sem=recv_sem.at[slot],
        device_id=device,
        device_id_type=pl.DeviceIdType.MESH,
    )


def meet(peers):
    barrier = pltpu.get_barrier_semaphore()
    for peer in peers:
        pl.semaphore_signal(barrier, inc=1, device_id=peer, device_id_type=pl.DeviceIdType.MESH)
    pl.semaphore_wait(barrier, len(peers))


def experts_kernel(
    normed_ref,
    placing_ref,
    placed_ref,
    w_in_ref,
    w_out_ref,
    tow1_ref,
    tow2_ref,
    targets_ref,
    predicted_ref,
    normed_grad_ref,
    grad_in_ref,
    grad_out_ref,
    outgoing,
    rows,
    partial,
    theirs,
    total,
    arrived,
    hidden,
    slope,
    grad_pre,
    send_sem,
    recv_sem,
):
    owners, capacity, width = outgoing.shape[1:]
    count = owners * capacity
    row, column = here()
    sibling = (row, 1 - column)
    peers = [(lax.rem(row + step, owners), column) for step in range(1, owners)]
    units = w_in_ref.shape[1]
    tile = 512
    contract_rows = (((0,), (0,)), ((), ()))
    contract_cols = (((1,), (1,)), ((), ()))
    sent = []

    def product(left, right, dims=(((1,), (0,)), ((), ()))):
        return lax.dot_general(left, right, dims, preferred_element_type=jnp.float32)

    def part(step):
        return pl.ds(pl.multiple_of(step * tile, tile), tile)

    def send(src, dst, slot, device):
        copy = remote(src, dst, send_sem, recv_sem, slot, device)
        copy.start()
        sent.append(copy)
        return copy

    def route(way, values, first):
        outgoing[way] = (
            product(placing_ref[...], values)
            .astype(jnp.bfloat16)
            .reshape(owners, capacity, width)
        )
        if first:
            meet(peers + [sibling])
        copies = [
            send(outgoing.at[way, peer[0]], rows.at[way, column, row], way * 2 * owners + i, peer)
            for i, peer in enumerate(peers)
        ]
        rows[way, column, row] = outgoing[way, row]
        for copy in copies:
            copy.wait_recv()
        return send(
            rows.at[way, column],
            rows.at[way, column],
            way * 2 * owners + owners - 1,
            sibling,
        )

    def give_back(way, between, after):
        base = (way * 2 + 1) * owners
        across = send(partial.at[way, 1 - column], theirs.at[way], base + owners - 1, sibling)
        between()
        across.wait_recv()
        total[way] = (
            partial[way, column].astype(jnp.float32) + theirs[way].astype(jnp.float32)
        ).astype(jnp.bfloat16)
        copies = [
            send(total.at[way, peer[0]], arrived.at[way, row], base + i, peer)
            for i, peer in enumerate(peers)
        ]
        arrived[way, row] = total[way, row]
        after()
        for copy in copies:
            copy.wait_recv()
        return product(placed_ref[...], arrived[way].reshape(count, width))

    def forward(block):
        values = rows[0, block].reshape(count, width)

        def step(i, summed):
            pre_act = product(values, w_in_ref[:, part(i)])
            sigma = jax.nn.sigmoid(pre_act)
            active = (pre_act * sigma).astype(jnp.bfloat16)
            hidden[block, :, part(i)] = active
            slope[block, :, part(i)] = sigma * (1.0 + pre_act * (1.0 - sigma))
            return summed + product(active, w_out_ref[part(i), :])

        summed = lax.fori_loop(0, units // tile, step, jnp.zeros((count, width), jnp.float32))
        partial[0, block] = summed.astype(jnp.bfloat16).reshape(owners, capacity, width)

    def backward(block):
        values = rows[1, block].reshape(count, width)

        def step(i, summed):
            change = product(values, w_out_ref[part(i), :], contract_cols)
            change = (change * slope[block, :, part(i)]).astype(jnp.bfloat16)
            grad_pre[block, :, part(i)] = change
            return summed + product(change, w_in_ref[:, part(i)], contract_cols)

        summed = lax.fori_loop(0, units // tile, step, jnp.zeros((count, width), jnp.float32))
        partial[1, block] = summed.astype(jnp.bfloat16).reshape(owners, capacity, width)

    def grads_out():
        values = rows[1].reshape(2 * count, width)

        def step(i, carry):
            units_of = hidden[:, :, part(i)].reshape(2 * count, tile)
            grad_out_ref[part(i), :] = product(units_of, values, contract_rows)
            return carry

        lax.fori_loop(0, units // tile, step, 0)

    def grads_in():
        values = rows[0].reshape(2 * count, width)

        def step(i, carry):
            change = grad_pre[:, :, part(i)].reshape(2 * count, tile)
            grad_in_ref[:, part(i)] = product(values, change, contract_rows)
            return carry

        lax.fori_loop(0, units // tile, step, 0)

    def nothing():
        return None

    across = route(0, normed_ref[...], True)
    forward(column)
    across.wait_recv()
    forward(1 - column)
    mixture = give_back(0, nothing, nothing)
    joined = (normed_ref[...].astype(jnp.float32) + mixture).astype(jnp.bfloat16)
    joined_grad = jnp.zeros(joined.shape, jnp.float32)
    for k in range(3):
        tower_pre = product(joined, tow1_ref[k])
        sigma = jax.nn.sigmoid(tower_pre)
        gain = tow2_ref[k : k + 1, :]
        logit = jnp.sum(tower_pre * sigma * gain, axis=-1, keepdims=True)
        guess = jax.nn.sigmoid(logit) if k < 2 else logit
        predicted_ref[:, k : k + 1] = guess
        tower_slope = sigma * (1.0 + tower_pre * (1.0 - sigma))
        tower_grad = ((guess - targets_ref[:, k : k + 1]) * gain * tower_slope).astype(jnp.bfloat16)
        joined_grad += product(tower_grad, tow1_ref[k], contract_cols)
    joined_grad = joined_grad.astype(jnp.bfloat16)
    across = route(1, joined_grad, False)
    backward(column)
    across.wait_recv()
    backward(1 - column)
    mixture_grad = give_back(1, grads_out, grads_in)
    normed_grad_ref[...] = joined_grad.astype(jnp.float32) + mixture_grad
    for copy in sent:
        copy.wait_send()


def run_experts(normed, placing, weight_in, weight_out, w_tow1, w_tow2, targets, capacity):
    owners = lax.axis_size("table")
    width, units = weight_in.shape
    block = (owners, capacity, width)
    count = owners * capacity
    operands = (normed, placing, placing.T, weight_in, weight_out, w_tow1, w_tow2, targets)
    return pl.pallas_call(
        experts_kernel,
        out_shape=[
            jax.ShapeDtypeStruct(targets.shape, jnp.float32),
            jax.ShapeDtypeStruct(normed.shape, jnp.float32),
            jax.ShapeDtypeStruct(weight_in.shape, jnp.float32),
            jax.ShapeDtypeStruct(weight_out.shape, jnp.float32),
        ],
        in_specs=[pl.BlockSpec(memory_space=pltpu.VMEM)] * len(operands),
        out_specs=[pl.BlockSpec(memory_space=pltpu.VMEM)] * 4,
        scratch_shapes=[
            pltpu.VMEM((2,) + block, jnp.bfloat16),
            pltpu.VMEM((2, 2) + block, jnp.bfloat16),
            pltpu.VMEM((2, 2) + block, jnp.bfloat16),
            pltpu.VMEM((2,) + block, jnp.bfloat16),
            pltpu.VMEM((2,) + block, jnp.bfloat16),
            pltpu.VMEM((2,) + block, jnp.bfloat16),
            pltpu.VMEM((2, count, units), jnp.bfloat16),
            pltpu.VMEM((2, count, units), jnp.float32),
            pltpu.VMEM((2, count, units), jnp.bfloat16),
            pltpu.SemaphoreType.DMA((4 * owners,)),
            pltpu.SemaphoreType.DMA((4 * owners,)),
        ],
        compiler_params=pltpu.CompilerParams(
            collective_id=1, has_side_effects=True, vmem_limit_bytes=40 << 20
        ),
    )(*operands)


def plane_of(row):
    layer, y, x = lax.div(row, 4), lax.rem(lax.div(row, 2), 2), lax.rem(row, 2)
    return layer, y, x


def place(layer, y, x):
    return layer * 4 + y * 2 + x


def scatter_kernel(x_ref, o_ref, diagonal, staged, arrived, up, down, send_sem, recv_sem):
    row, column = here()
    z, y, x = plane_of(row)
    beside, above = (place(z, y, 1 - x), column), (place(z, 1 - y, x), column)
    layers = [lax.rem(z + s, 4) for s in range(4)]
    meet([beside, above] + [(place(layers[s], y, x), column) for s in (1, 2, 3)])
    half = x_ref.shape[1] // 2
    first, last = pl.ds(0, half), pl.ds(half, half)
    turns = (2, 1, 3, 0)
    sent = []
    corner = {}
    for s in turns:
        target = x_ref.at[place(layers[s], 1 - y, 1 - x)]
        corner[s] = (
            remote(target.at[first], diagonal.at[s, 0], send_sem, recv_sem, s * 5, beside),
            remote(target.at[last], diagonal.at[s, 1], send_sem, recv_sem, s * 5 + 1, above),
        )
        for copy in corner[s]:
            copy.start()
            sent.append(copy)
    side = {}
    for s in turns:
        to_beside, to_above = place(layers[s], y, 1 - x), place(layers[s], 1 - y, x)
        corner[s][0].wait_recv()
        staged[s, 1, first] = (
            x_ref[to_above, first].astype(jnp.float32) + diagonal[s, 0].astype(jnp.float32)
        ).astype(staged.dtype)
        staged[s, 1, last] = x_ref[to_above, last]
        corner[s][1].wait_recv()
        staged[s, 0, first] = x_ref[to_beside, first]
        staged[s, 0, last] = (
            x_ref[to_beside, last].astype(jnp.float32) + diagonal[s, 1].astype(jnp.float32)
        ).astype(staged.dtype)
        side[s] = (
            remote(staged.at[s, 0], arrived.at[s, 0], send_sem, recv_sem, s * 5 + 2, beside),
            remote(staged.at[s, 1], arrived.at[s, 1], send_sem, recv_sem, s * 5 + 3, above),
        )
        for copy in side[s]:
            copy.start()
            sent.append(copy)
    vertical = {}
    for s in turns:
        for copy in side[s]:
            copy.wait_recv()
        partial = (
            x_ref[place(layers[s], y, x)].astype(jnp.float32)
            + arrived[s, 0].astype(jnp.float32)
            + arrived[s, 1].astype(jnp.float32)
        )
        if s == 0:
            o_ref[...] = partial
        else:
            up[s] = partial.astype(up.dtype)
            vertical[s] = remote(
                up.at[s], down.at[s], send_sem, recv_sem, s * 5 + 4, (place(layers[s], y, x), column)
            )
            vertical[s].start()
            sent.append(vertical[s])
    for s in turns[:3]:
        vertical[s].wait_recv()
        o_ref[...] += down[s].astype(jnp.float32)
    for copy in sent:
        copy.wait_send()


def gather_kernel(x_ref, o_ref, send_sem, recv_sem, own_sem):
    row, column = here()
    z, y, x = plane_of(row)
    beside, above = (place(z, y, 1 - x), column), (place(z, 1 - y, x), column)
    own = pltpu.make_async_copy(x_ref, o_ref.at[row], own_sem)
    own.start()
    meet([beside, above] + [(place(lax.rem(z + s, 4), y, x), column) for s in (1, 2, 3)])
    half = x_ref.shape[0] // 2
    first, last = pl.ds(0, half), pl.ds(half, half)
    sent = []

    def send(src, dst, slot, device):
        copy = remote(src, dst, send_sem, recv_sem, slot, device)
        copy.start()
        sent.append(copy)
        return copy

    vertical = {
        s: send(x_ref, o_ref.at[row], s * 5, (place(lax.rem(z + s, 4), y, x), column))
        for s in (1, 3, 2)
    }
    turns = (0, 1, 3, 2)
    side = {}
    for s in turns:
        mine = place(lax.rem(z + 4 - s, 4), y, x)
        source = x_ref
        if s > 0:
            vertical[s].wait_recv()
            source = o_ref.at[mine]
        side[s] = (
            send(source, o_ref.at[mine], s * 5 + 1, beside),
            send(source, o_ref.at[mine], s * 5 + 2, above),
        )
    corner = []
    for s in turns:
        layer = lax.rem(z + 4 - s, 4)
        side[s][0].wait_recv()
        block = o_ref.at[place(layer, y, 1 - x), first]
        corner.append(send(block, block, s * 5 + 3, above))
        side[s][1].wait_recv()
        block = o_ref.at[place(layer, 1 - y, x), last]
        corner.append(send(block, block, s * 5 + 4, beside))
    for copy in corner:
        copy.wait_recv()
    own.wait()
    for copy in sent:
        copy.wait_send()


def call(kernel, operand, shape, dtype, scratch, copies, collective_id):
    semaphores = [pltpu.SemaphoreType.DMA((copies,)), pltpu.SemaphoreType.DMA((copies,))]
    return pl.pallas_call(
        kernel,
        out_shape=jax.ShapeDtypeStruct(shape, dtype),
        in_specs=[pl.BlockSpec(memory_space=pltpu.VMEM)],
        out_specs=pl.BlockSpec(memory_space=pltpu.VMEM),
        scratch_shapes=[pltpu.VMEM(s, jnp.bfloat16) for s in scratch] + semaphores
        + ([] if kernel is scatter_kernel else [pltpu.SemaphoreType.DMA]),
        compiler_params=pltpu.CompilerParams(
            collective_id=collective_id, has_side_effects=True, vmem_limit_bytes=32 << 20
        ),
    )(operand)


def direct():
    return lax.axis_size("expert") == 2 and lax.axis_size("table") == 16


def dispatch(buffer):
    arrived = lax.all_to_all(buffer, "table", split_axis=0, concat_axis=0, tiled=True)
    columns = lax.all_gather(arrived[None], "expert", axis=0, tiled=True)
    return columns.reshape(-1, buffer.shape[-1])


def send_back(partial, experts, capacity):
    width = partial.shape[-1]
    partial = partial.astype(jnp.bfloat16)
    summed = lax.psum_scatter(partial, "expert", scatter_dimension=0, tiled=True)
    arrived = lax.all_to_all(
        summed.reshape(experts, capacity, width), "table", split_axis=0, concat_axis=0, tiled=True
    )
    return arrived.reshape(experts * capacity, width)


def sum_features(weighted, samples):
    width = weighted.shape[-1]
    if direct():
        block = (samples, width)
        return call(
            scatter_kernel,
            weighted.reshape(-1, samples, width),
            block,
            jnp.float32,
            ((4, 2, samples // 2, width), (4, 2) + block, (4, 2) + block, (4,) + block, (4,) + block),
            20,
            5,
        )
    return lax.psum_scatter(weighted, "table", scatter_dimension=0, tiled=True).astype(jnp.float32)


def gather_rows(rows):
    if direct():
        owners = lax.axis_size("table")
        gathered = call(gather_kernel, rows, (owners,) + rows.shape, rows.dtype, (), 20, 6)
        return gathered.reshape(-1, rows.shape[-1])
    return lax.all_gather(rows, "table", axis=0, tiled=True)


def sum_rows(row_grad):
    row_grad = row_grad.astype(jnp.bfloat16)
    if direct():
        half = row_grad.shape[0] // 2
        column = lax.axis_index("expert")
        theirs = lax.dynamic_slice_in_dim(row_grad, (1 - column) * half, half, 0)
        ours = lax.dynamic_slice_in_dim(row_grad, column * half, half, 0)
        arrived = lax.ppermute(theirs, "expert", [(0, 1), (1, 0)])
        return ours.astype(jnp.float32) + arrived.astype(jnp.float32)
    return lax.psum_scatter(row_grad, "expert", scatter_dimension=0, tiled=True).astype(jnp.float32)


def route_experts(normed, placing, weight_in, weight_out, w_tow1, w_tow2, targets, capacity):
    owners = lax.axis_size("table")
    contract_rows = (((0,), (0,)), ((), ()))
    contract_cols = (((1,), (1,)), ((), ()))
    outgoing = jnp.dot(placing, normed, preferred_element_type=jnp.float32).astype(jnp.bfloat16)
    gathered = dispatch(outgoing.reshape(owners, capacity, outgoing.shape[-1]))
    pre_act = jnp.dot(gathered, weight_in, preferred_element_type=jnp.float32)
    hidden = jax.nn.silu(pre_act).astype(jnp.bfloat16)

    forward = jnp.dot(hidden, weight_out, preferred_element_type=jnp.float32)
    expert_out = send_back(forward, owners, capacity)
    mixture = lax.dot_general(
        placing, expert_out, contract_rows, preferred_element_type=jnp.float32
    )
    joined = (normed.astype(jnp.float32) + mixture).astype(jnp.bfloat16)
    tower_pre = jnp.einsum("be,kem->kbm", joined, w_tow1, preferred_element_type=jnp.float32)
    logits = jnp.sum(jax.nn.silu(tower_pre) * w_tow2[:, None, :], axis=-1)
    predicted = jnp.stack(
        [jax.nn.sigmoid(logits[0]), jax.nn.sigmoid(logits[1]), logits[2]], axis=-1
    )
    logit_grad = predicted - targets
    tower_grad = (logit_grad.T[:, :, None] * w_tow2[:, None, :] * silu_slope(tower_pre)).astype(
        jnp.bfloat16
    )
    joined_grad = jnp.einsum(
        "kbm,kem->be", tower_grad, w_tow1, preferred_element_type=jnp.float32
    ).astype(jnp.bfloat16)
    back_rows = jnp.dot(placing, joined_grad, preferred_element_type=jnp.float32).astype(
        jnp.bfloat16
    )
    gathered_grad = dispatch(back_rows.reshape(owners, capacity, back_rows.shape[-1]))
    grad_hidden = lax.dot_general(
        gathered_grad, weight_out, contract_cols, preferred_element_type=jnp.float32
    )
    grad_pre = (grad_hidden * silu_slope(pre_act)).astype(jnp.bfloat16)
    grad_out = lax.dot_general(
        hidden, gathered_grad, contract_rows, preferred_element_type=jnp.float32
    )
    grad_in = lax.dot_general(gathered, grad_pre, contract_rows, preferred_element_type=jnp.float32)

    backward = lax.dot_general(
        grad_pre, weight_in, contract_cols, preferred_element_type=jnp.float32
    )
    input_grad = send_back(backward, owners, capacity)
    mixture_grad = lax.dot_general(
        placing, input_grad, contract_rows, preferred_element_type=jnp.float32
    )
    normed_grad = joined_grad.astype(jnp.float32) + mixture_grad
    return predicted, normed_grad, grad_in, grad_out


def local(
    table,
    row_scale,
    windows,
    bag_idx,
    bag_len,
    feat_gain,
    norm_gain,
    expert_ids,
    w_in,
    w_out,
    w_tow1,
    w_tow2,
    targets,
):
    owners = lax.axis_size("table")
    samples = expert_ids.shape[1]
    capacity = max(2, 2 * samples // owners)
    local_rows = owners * capacity
    contract_rows = (((0,), (0,)), ((), ()))
    window = windows[0, 0]
    row_select = (
        jnp.arange(table.shape[1], dtype=jnp.int32)[:, None] == window[None, :]
    ).astype(jnp.bfloat16)
    rows = (table[0].astype(jnp.float32) * row_scale[0][:, None] / code_range).astype(jnp.bfloat16)
    dequant = lax.dot_general(
        row_select, rows, contract_rows, preferred_element_type=jnp.float32
    ).astype(jnp.bfloat16)
    counts = bag_counts(bag_idx[0, 0], bag_len[0, 0], window.shape[0])
    pooled = lax.dot_general(counts, dequant, contract_rows, preferred_element_type=jnp.float32)
    own_gain = lax.dynamic_slice_in_dim(feat_gain, lax.axis_index("table"), 1, 0)
    weighted = (pooled.astype(jnp.bfloat16).astype(jnp.float32) * own_gain).astype(jnp.bfloat16)
    summed = sum_features(weighted, samples)
    inverse = lax.rsqrt(jnp.mean(summed * summed, axis=-1, keepdims=True) + 1e-05)
    normed = (summed * inverse * norm_gain).astype(jnp.bfloat16)
    chosen = expert_ids[0, :, 0]
    member = (chosen[:, None] == jnp.arange(owners, dtype=jnp.int32)[None, :]).astype(jnp.bfloat16)
    order = jnp.arange(samples, dtype=jnp.int32)
    earlier = (order[None, :] < order[:, None]).astype(jnp.bfloat16)
    ranks = jnp.dot(earlier, member, preferred_element_type=jnp.float32)
    slot_of = jnp.sum(ranks * member.astype(jnp.float32), axis=1).astype(jnp.int32)
    target_slot = chosen * capacity + slot_of
    placing = (jnp.arange(local_rows, dtype=jnp.int32)[:, None] == target_slot[None, :]).astype(
        jnp.bfloat16
    )
    run = run_experts if direct() else route_experts
    predicted, normed_grad, grad_in, grad_out = run(
        normed, placing, w_in[0], w_out[0], w_tow1, w_tow2, targets[0], capacity
    )
    scaled_grad = normed_grad * norm_gain
    summed_grad = inverse * (
        scaled_grad
        - summed * inverse * inverse * jnp.mean(scaled_grad * summed, axis=-1, keepdims=True)
    )
    returned = gather_rows(summed_grad.astype(jnp.bfloat16))
    window_grad = jnp.dot(counts, returned, preferred_element_type=jnp.float32) * own_gain
    row_grad = jnp.dot(
        row_select, window_grad.astype(jnp.bfloat16), preferred_element_type=jnp.float32
    )
    table_grad = sum_rows(row_grad)
    return (predicted[None], table_grad[None], grad_in[None], grad_out[None])


def solution(mesh):
    in_specs = (
        P("table", None, None),
        P("table", None),
        P("table", "expert", None),
        P("table", "expert", None, None),
        P("table", "expert", None),
        P(),
        P(),
        P("expert", "table", None),
        P("table", None, "expert"),
        P("table", "expert", None),
        P(),
        P(),
        P("expert", "table", None),
    )
    out_specs = (
        P("expert", "table", None),
        P("table", "expert", None),
        P("table", None, "expert"),
        P("table", "expert", None),
    )
    return jax.shard_map(local, mesh=mesh, in_specs=in_specs, out_specs=out_specs, check_vma=False)
```

```python
import functools

import jax
import jax.numpy as jnp
from jax import lax
from jax.experimental import pallas as pl
from jax.experimental.pallas import tpu as pltpu
from jax.sharding import PartitionSpec as P

code_range = 127.0


def silu_slope(values):
    sigma = jax.nn.sigmoid(values)
    return sigma * (1.0 + values * (1.0 - sigma))


def bag_counts(indices, lengths, window):
    slots = jnp.arange(indices.shape[1], dtype=jnp.int32)
    live = jnp.where(slots[:, None] < lengths[None, :], indices.T, -1)
    positions = jnp.arange(window, dtype=jnp.int32)
    hits = (live[:, None, :] == positions[None, :, None]).astype(jnp.float32)
    return jnp.sum(hits, axis=0).astype(jnp.bfloat16)


def here():
    return lax.axis_index("table"), lax.axis_index("expert")


def remote(src, dst, send_sem, recv_sem, slot, device):
    return pltpu.make_async_remote_copy(
        src_ref=src,
        dst_ref=dst,
        send_sem=send_sem.at[slot],
        recv_sem=recv_sem.at[slot],
        device_id=device,
        device_id_type=pl.DeviceIdType.MESH,
    )


def meet(peers):
    barrier = pltpu.get_barrier_semaphore()
    for peer in peers:
        pl.semaphore_signal(barrier, inc=1, device_id=peer, device_id_type=pl.DeviceIdType.MESH)
    pl.semaphore_wait(barrier, len(peers))


def experts_kernel(
    normed_ref,
    placing_ref,
    placed_ref,
    w_in_far,
    w_out_far,
    tow1_far,
    tow2_ref,
    targets_ref,
    predicted_ref,
    normed_grad_ref,
    grad_in_ref,
    grad_out_ref,
    outgoing,
    rows,
    partial,
    theirs,
    total,
    arrived,
    hidden,
    slope,
    grad_pre,
    w_in_ref,
    w_out_ref,
    tow1_ref,
    send_sem,
    recv_sem,
    load_sem,
):
    owners, capacity, width = outgoing.shape[1:]
    count = owners * capacity
    row, column = here()
    sibling = (row, 1 - column)
    peers = [(lax.rem(row + step, owners), column) for step in range(1, owners)]
    units = w_in_ref.shape[1]
    tile = 512
    contract_rows = (((0,), (0,)), ((), ()))
    contract_cols = (((1,), (1,)), ((), ()))
    sent = []

    def product(left, right, dims=(((1,), (0,)), ((), ()))):
        return lax.dot_general(left, right, dims, preferred_element_type=jnp.float32)

    def part(step):
        return pl.ds(pl.multiple_of(step * tile, tile), tile)

    def send(src, dst, slot, device):
        copy = remote(src, dst, send_sem, recv_sem, slot, device)
        copy.start()
        sent.append(copy)
        return copy

    def route(way, values, first):
        outgoing[way] = (
            product(placing_ref[...], values)
            .astype(jnp.bfloat16)
            .reshape(owners, capacity, width)
        )
        if first:
            meet(peers + [sibling])
        copies = [
            send(outgoing.at[way, peer[0]], rows.at[way, column, row], way * 2 * owners + i, peer)
            for i, peer in enumerate(peers)
        ]
        rows[way, column, row] = outgoing[way, row]
        for copy in copies:
            copy.wait_recv()
        return send(
            rows.at[way, column],
            rows.at[way, column],
            way * 2 * owners + owners - 1,
            sibling,
        )

    def give_back(way, between, after):
        base = (way * 2 + 1) * owners
        across = send(partial.at[way, 1 - column], theirs.at[way], base + owners - 1, sibling)
        between()
        across.wait_recv()
        total[way] = (
            partial[way, column].astype(jnp.float32) + theirs[way].astype(jnp.float32)
        ).astype(jnp.bfloat16)
        copies = [
            send(total.at[way, peer[0]], arrived.at[way, row], base + i, peer)
            for i, peer in enumerate(peers)
        ]
        arrived[way, row] = total[way, row]
        after()
        for copy in copies:
            copy.wait_recv()
        return product(placed_ref[...], arrived[way].reshape(count, width))

    def forward(block):
        values = rows[0, block].reshape(count, width)

        def step(i, summed):
            pre_act = product(values, w_in_ref[:, part(i)])
            sigma = jax.nn.sigmoid(pre_act)
            active = (pre_act * sigma).astype(jnp.bfloat16)
            hidden[block, :, part(i)] = active
            slope[block, :, part(i)] = sigma * (1.0 + pre_act * (1.0 - sigma))
            return summed + product(active, w_out_ref[part(i), :])

        summed = lax.fori_loop(0, units // tile, step, jnp.zeros((count, width), jnp.float32))
        partial[0, block] = summed.astype(jnp.bfloat16).reshape(owners, capacity, width)

    def backward(block):
        values = rows[1, block].reshape(count, width)

        def step(i, summed):
            change = product(values, w_out_ref[part(i), :], contract_cols)
            change = (change * slope[block, :, part(i)]).astype(jnp.bfloat16)
            grad_pre[block, :, part(i)] = change
            return summed + product(change, w_in_ref[:, part(i)], contract_cols)

        summed = lax.fori_loop(0, units // tile, step, jnp.zeros((count, width), jnp.float32))
        partial[1, block] = summed.astype(jnp.bfloat16).reshape(owners, capacity, width)

    def grads_out():
        values = rows[1].reshape(2 * count, width)

        def step(i, carry):
            units_of = hidden[:, :, part(i)].reshape(2 * count, tile)
            grad_out_ref[part(i), :] = product(units_of, values, contract_rows)
            return carry

        lax.fori_loop(0, units // tile, step, 0)

    def grads_in():
        values = rows[0].reshape(2 * count, width)

        def step(i, carry):
            change = grad_pre[:, :, part(i)].reshape(2 * count, tile)
            grad_in_ref[:, part(i)] = product(values, change, contract_rows)
            return carry

        lax.fori_loop(0, units // tile, step, 0)

    def nothing():
        return None

    loads = [
        pltpu.make_async_copy(far, near, load_sem.at[i])
        for i, (far, near) in enumerate(
            ((w_in_far, w_in_ref), (w_out_far, w_out_ref), (tow1_far, tow1_ref))
        )
    ]
    for load in loads:
        load.start()
    across = route(0, normed_ref[...], True)
    for load in loads:
        load.wait()
    forward(column)
    across.wait_recv()
    forward(1 - column)
    mixture = give_back(0, nothing, nothing)
    joined = (normed_ref[...].astype(jnp.float32) + mixture).astype(jnp.bfloat16)
    joined_grad = jnp.zeros(joined.shape, jnp.float32)
    for k in range(3):
        tower_pre = product(joined, tow1_ref[k])
        sigma = jax.nn.sigmoid(tower_pre)
        gain = tow2_ref[k : k + 1, :]
        logit = jnp.sum(tower_pre * sigma * gain, axis=-1, keepdims=True)
        guess = jax.nn.sigmoid(logit) if k < 2 else logit
        predicted_ref[:, k : k + 1] = guess
        tower_slope = sigma * (1.0 + tower_pre * (1.0 - sigma))
        tower_grad = ((guess - targets_ref[:, k : k + 1]) * gain * tower_slope).astype(jnp.bfloat16)
        joined_grad += product(tower_grad, tow1_ref[k], contract_cols)
    joined_grad = joined_grad.astype(jnp.bfloat16)
    across = route(1, joined_grad, False)
    backward(column)
    across.wait_recv()
    backward(1 - column)
    mixture_grad = give_back(1, grads_out, grads_in)
    normed_grad_ref[...] = joined_grad.astype(jnp.float32) + mixture_grad
    for copy in sent:
        copy.wait_send()


def run_experts(normed, placing, weight_in, weight_out, w_tow1, w_tow2, targets, capacity):
    owners = lax.axis_size("table")
    width, units = weight_in.shape
    block = (owners, capacity, width)
    count = owners * capacity
    operands = (normed, placing, placing.T, weight_in, weight_out, w_tow1, w_tow2, targets)
    return pl.pallas_call(
        experts_kernel,
        out_shape=[
            jax.ShapeDtypeStruct(targets.shape, jnp.float32),
            jax.ShapeDtypeStruct(normed.shape, jnp.float32),
            jax.ShapeDtypeStruct(weight_in.shape, jnp.float32),
            jax.ShapeDtypeStruct(weight_out.shape, jnp.float32),
        ],
        in_specs=[
            pl.BlockSpec(memory_space=pl.ANY if i in (3, 4, 5) else pltpu.VMEM)
            for i in range(len(operands))
        ],
        out_specs=[pl.BlockSpec(memory_space=pltpu.VMEM)] * 4,
        scratch_shapes=[
            pltpu.VMEM((2,) + block, jnp.bfloat16),
            pltpu.VMEM((2, 2) + block, jnp.bfloat16),
            pltpu.VMEM((2, 2) + block, jnp.bfloat16),
            pltpu.VMEM((2,) + block, jnp.bfloat16),
            pltpu.VMEM((2,) + block, jnp.bfloat16),
            pltpu.VMEM((2,) + block, jnp.bfloat16),
            pltpu.VMEM((2, count, units), jnp.bfloat16),
            pltpu.VMEM((2, count, units), jnp.float32),
            pltpu.VMEM((2, count, units), jnp.bfloat16),
            pltpu.VMEM(weight_in.shape, weight_in.dtype),
            pltpu.VMEM(weight_out.shape, weight_out.dtype),
            pltpu.VMEM(w_tow1.shape, w_tow1.dtype),
            pltpu.SemaphoreType.DMA((4 * owners,)),
            pltpu.SemaphoreType.DMA((4 * owners,)),
            pltpu.SemaphoreType.DMA((3,)),
        ],
        compiler_params=pltpu.CompilerParams(
            collective_id=1, has_side_effects=True, vmem_limit_bytes=60 << 20
        ),
    )(*operands)


def plane_of(row):
    layer, y, x = lax.div(row, 4), lax.rem(lax.div(row, 2), 2), lax.rem(row, 2)
    return layer, y, x


def place(layer, y, x):
    return layer * 4 + y * 2 + x


def scatter_kernel(x_ref, o_ref, diagonal, staged, arrived, up, down, send_sem, recv_sem):
    row, column = here()
    z, y, x = plane_of(row)
    beside, above = (place(z, y, 1 - x), column), (place(z, 1 - y, x), column)
    layers = [lax.rem(z + s, 4) for s in range(4)]
    meet([beside, above] + [(place(layers[s], y, x), column) for s in (1, 2, 3)])
    half = x_ref.shape[1] // 2
    first, last = pl.ds(0, half), pl.ds(half, half)
    turns = (2, 1, 3, 0)
    sent = []
    corner = {}
    for s in turns:
        target = x_ref.at[place(layers[s], 1 - y, 1 - x)]
        corner[s] = (
            remote(target.at[first], diagonal.at[s, 0], send_sem, recv_sem, s * 5, beside),
            remote(target.at[last], diagonal.at[s, 1], send_sem, recv_sem, s * 5 + 1, above),
        )
        for copy in corner[s]:
            copy.start()
            sent.append(copy)
    side = {}
    for s in turns:
        to_beside, to_above = place(layers[s], y, 1 - x), place(layers[s], 1 - y, x)
        corner[s][0].wait_recv()
        staged[s, 1, first] = (
            x_ref[to_above, first].astype(jnp.float32) + diagonal[s, 0].astype(jnp.float32)
        ).astype(staged.dtype)
        staged[s, 1, last] = x_ref[to_above, last]
        corner[s][1].wait_recv()
        staged[s, 0, first] = x_ref[to_beside, first]
        staged[s, 0, last] = (
            x_ref[to_beside, last].astype(jnp.float32) + diagonal[s, 1].astype(jnp.float32)
        ).astype(staged.dtype)
        side[s] = (
            remote(staged.at[s, 0], arrived.at[s, 0], send_sem, recv_sem, s * 5 + 2, beside),
            remote(staged.at[s, 1], arrived.at[s, 1], send_sem, recv_sem, s * 5 + 3, above),
        )
        for copy in side[s]:
            copy.start()
            sent.append(copy)
    vertical = {}
    for s in turns:
        for copy in side[s]:
            copy.wait_recv()
        partial = (
            x_ref[place(layers[s], y, x)].astype(jnp.float32)
            + arrived[s, 0].astype(jnp.float32)
            + arrived[s, 1].astype(jnp.float32)
        )
        if s == 0:
            o_ref[...] = partial
        else:
            up[s] = partial.astype(up.dtype)
            vertical[s] = remote(
                up.at[s], down.at[s], send_sem, recv_sem, s * 5 + 4, (place(layers[s], y, x), column)
            )
            vertical[s].start()
            sent.append(vertical[s])
    for s in turns[:3]:
        vertical[s].wait_recv()
        o_ref[...] += down[s].astype(jnp.float32)
    for copy in sent:
        copy.wait_send()


def gather_kernel(x_ref, o_ref, send_sem, recv_sem, own_sem):
    row, column = here()
    z, y, x = plane_of(row)
    beside, above = (place(z, y, 1 - x), column), (place(z, 1 - y, x), column)
    own = pltpu.make_async_copy(x_ref, o_ref.at[row], own_sem)
    own.start()
    meet([beside, above] + [(place(lax.rem(z + s, 4), y, x), column) for s in (1, 2, 3)])
    half = x_ref.shape[0] // 2
    first, last = pl.ds(0, half), pl.ds(half, half)
    sent = []

    def send(src, dst, slot, device):
        copy = remote(src, dst, send_sem, recv_sem, slot, device)
        copy.start()
        sent.append(copy)
        return copy

    vertical = {
        s: send(x_ref, o_ref.at[row], s * 5, (place(lax.rem(z + s, 4), y, x), column))
        for s in (1, 3, 2)
    }
    turns = (0, 1, 3, 2)
    side = {}
    for s in turns:
        mine = place(lax.rem(z + 4 - s, 4), y, x)
        source = x_ref
        if s > 0:
            vertical[s].wait_recv()
            source = o_ref.at[mine]
        side[s] = (
            send(source, o_ref.at[mine], s * 5 + 1, beside),
            send(source, o_ref.at[mine], s * 5 + 2, above),
        )
    corner = []
    for s in turns:
        layer = lax.rem(z + 4 - s, 4)
        side[s][0].wait_recv()
        block = o_ref.at[place(layer, y, 1 - x), first]
        corner.append(send(block, block, s * 5 + 3, above))
        side[s][1].wait_recv()
        block = o_ref.at[place(layer, 1 - y, x), last]
        corner.append(send(block, block, s * 5 + 4, beside))
    for copy in corner:
        copy.wait_recv()
    own.wait()
    for copy in sent:
        copy.wait_send()


def call(kernel, operand, shape, dtype, scratch, copies, collective_id):
    semaphores = [pltpu.SemaphoreType.DMA((copies,)), pltpu.SemaphoreType.DMA((copies,))]
    return pl.pallas_call(
        kernel,
        out_shape=jax.ShapeDtypeStruct(shape, dtype),
        in_specs=[pl.BlockSpec(memory_space=pltpu.VMEM)],
        out_specs=pl.BlockSpec(memory_space=pltpu.VMEM),
        scratch_shapes=[pltpu.VMEM(s, jnp.bfloat16) for s in scratch] + semaphores
        + ([] if kernel is scatter_kernel else [pltpu.SemaphoreType.DMA]),
        compiler_params=pltpu.CompilerParams(
            collective_id=collective_id, has_side_effects=True, vmem_limit_bytes=8 << 20
        ),
    )(operand)


def direct():
    return lax.axis_size("expert") == 2 and lax.axis_size("table") == 16


def dispatch(buffer):
    arrived = lax.all_to_all(buffer, "table", split_axis=0, concat_axis=0, tiled=True)
    columns = lax.all_gather(arrived[None], "expert", axis=0, tiled=True)
    return columns.reshape(-1, buffer.shape[-1])


def send_back(partial, experts, capacity):
    width = partial.shape[-1]
    partial = partial.astype(jnp.bfloat16)
    summed = lax.psum_scatter(partial, "expert", scatter_dimension=0, tiled=True)
    arrived = lax.all_to_all(
        summed.reshape(experts, capacity, width), "table", split_axis=0, concat_axis=0, tiled=True
    )
    return arrived.reshape(experts * capacity, width)


def sum_features(weighted, samples):
    width = weighted.shape[-1]
    if direct():
        block = (samples, width)
        return call(
            scatter_kernel,
            weighted.reshape(-1, samples, width),
            block,
            jnp.float32,
            ((4, 2, samples // 2, width), (4, 2) + block, (4, 2) + block, (4,) + block, (4,) + block),
            20,
            5,
        )
    return lax.psum_scatter(weighted, "table", scatter_dimension=0, tiled=True).astype(jnp.float32)


def gather_rows(rows):
    if direct():
        owners = lax.axis_size("table")
        gathered = call(gather_kernel, rows, (owners,) + rows.shape, rows.dtype, (), 20, 6)
        return gathered.reshape(-1, rows.shape[-1])
    return lax.all_gather(rows, "table", axis=0, tiled=True)


def sum_rows(row_grad):
    row_grad = row_grad.astype(jnp.bfloat16)
    if direct():
        half = row_grad.shape[0] // 2
        column = lax.axis_index("expert")
        theirs = lax.dynamic_slice_in_dim(row_grad, (1 - column) * half, half, 0)
        ours = lax.dynamic_slice_in_dim(row_grad, column * half, half, 0)
        arrived = lax.ppermute(theirs, "expert", [(0, 1), (1, 0)])
        return ours.astype(jnp.float32) + arrived.astype(jnp.float32)
    return lax.psum_scatter(row_grad, "expert", scatter_dimension=0, tiled=True).astype(jnp.float32)


def route_experts(normed, placing, weight_in, weight_out, w_tow1, w_tow2, targets, capacity):
    owners = lax.axis_size("table")
    contract_rows = (((0,), (0,)), ((), ()))
    contract_cols = (((1,), (1,)), ((), ()))
    outgoing = jnp.dot(placing, normed, preferred_element_type=jnp.float32).astype(jnp.bfloat16)
    gathered = dispatch(outgoing.reshape(owners, capacity, outgoing.shape[-1]))
    pre_act = jnp.dot(gathered, weight_in, preferred_element_type=jnp.float32)
    hidden = jax.nn.silu(pre_act).astype(jnp.bfloat16)

    forward = jnp.dot(hidden, weight_out, preferred_element_type=jnp.float32)
    expert_out = send_back(forward, owners, capacity)
    mixture = lax.dot_general(
        placing, expert_out, contract_rows, preferred_element_type=jnp.float32
    )
    joined = (normed.astype(jnp.float32) + mixture).astype(jnp.bfloat16)
    tower_pre = jnp.einsum("be,kem->kbm", joined, w_tow1, preferred_element_type=jnp.float32)
    logits = jnp.sum(jax.nn.silu(tower_pre) * w_tow2[:, None, :], axis=-1)
    predicted = jnp.stack(
        [jax.nn.sigmoid(logits[0]), jax.nn.sigmoid(logits[1]), logits[2]], axis=-1
    )
    logit_grad = predicted - targets
    tower_grad = (logit_grad.T[:, :, None] * w_tow2[:, None, :] * silu_slope(tower_pre)).astype(
        jnp.bfloat16
    )
    joined_grad = jnp.einsum(
        "kbm,kem->be", tower_grad, w_tow1, preferred_element_type=jnp.float32
    ).astype(jnp.bfloat16)
    back_rows = jnp.dot(placing, joined_grad, preferred_element_type=jnp.float32).astype(
        jnp.bfloat16
    )
    gathered_grad = dispatch(back_rows.reshape(owners, capacity, back_rows.shape[-1]))
    grad_hidden = lax.dot_general(
        gathered_grad, weight_out, contract_cols, preferred_element_type=jnp.float32
    )
    grad_pre = (grad_hidden * silu_slope(pre_act)).astype(jnp.bfloat16)
    grad_out = lax.dot_general(
        hidden, gathered_grad, contract_rows, preferred_element_type=jnp.float32
    )
    grad_in = lax.dot_general(gathered, grad_pre, contract_rows, preferred_element_type=jnp.float32)

    backward = lax.dot_general(
        grad_pre, weight_in, contract_cols, preferred_element_type=jnp.float32
    )
    input_grad = send_back(backward, owners, capacity)
    mixture_grad = lax.dot_general(
        placing, input_grad, contract_rows, preferred_element_type=jnp.float32
    )
    normed_grad = joined_grad.astype(jnp.float32) + mixture_grad
    return predicted, normed_grad, grad_in, grad_out


def local(
    table,
    row_scale,
    windows,
    bag_idx,
    bag_len,
    feat_gain,
    norm_gain,
    expert_ids,
    w_in,
    w_out,
    w_tow1,
    w_tow2,
    targets,
):
    owners = lax.axis_size("table")
    samples = expert_ids.shape[1]
    capacity = max(2, 2 * samples // owners)
    local_rows = owners * capacity
    contract_rows = (((0,), (0,)), ((), ()))
    window = windows[0, 0]
    row_select = (
        jnp.arange(table.shape[1], dtype=jnp.int32)[:, None] == window[None, :]
    ).astype(jnp.bfloat16)
    rows = (table[0].astype(jnp.float32) * row_scale[0][:, None] / code_range).astype(jnp.bfloat16)
    dequant = lax.dot_general(
        row_select, rows, contract_rows, preferred_element_type=jnp.float32
    ).astype(jnp.bfloat16)
    counts = bag_counts(bag_idx[0, 0], bag_len[0, 0], window.shape[0])
    pooled = lax.dot_general(counts, dequant, contract_rows, preferred_element_type=jnp.float32)
    own_gain = lax.dynamic_slice_in_dim(feat_gain, lax.axis_index("table"), 1, 0)
    weighted = (pooled.astype(jnp.bfloat16).astype(jnp.float32) * own_gain).astype(jnp.bfloat16)
    summed = sum_features(weighted, samples)
    inverse = lax.rsqrt(jnp.mean(summed * summed, axis=-1, keepdims=True) + 1e-05)
    normed = (summed * inverse * norm_gain).astype(jnp.bfloat16)
    chosen = expert_ids[0, :, 0]
    member = (chosen[:, None] == jnp.arange(owners, dtype=jnp.int32)[None, :]).astype(jnp.bfloat16)
    order = jnp.arange(samples, dtype=jnp.int32)
    earlier = (order[None, :] < order[:, None]).astype(jnp.bfloat16)
    ranks = jnp.dot(earlier, member, preferred_element_type=jnp.float32)
    slot_of = jnp.sum(ranks * member.astype(jnp.float32), axis=1).astype(jnp.int32)
    target_slot = chosen * capacity + slot_of
    placing = (jnp.arange(local_rows, dtype=jnp.int32)[:, None] == target_slot[None, :]).astype(
        jnp.bfloat16
    )
    run = run_experts if direct() else route_experts
    predicted, normed_grad, grad_in, grad_out = run(
        normed, placing, w_in[0], w_out[0], w_tow1, w_tow2, targets[0], capacity
    )
    scaled_grad = normed_grad * norm_gain
    summed_grad = inverse * (
        scaled_grad
        - summed * inverse * inverse * jnp.mean(scaled_grad * summed, axis=-1, keepdims=True)
    )
    returned = gather_rows(summed_grad.astype(jnp.bfloat16))
    window_grad = jnp.dot(counts, returned, preferred_element_type=jnp.float32) * own_gain
    row_grad = jnp.dot(
        row_select, window_grad.astype(jnp.bfloat16), preferred_element_type=jnp.float32
    )
    table_grad = sum_rows(row_grad)
    return (predicted[None], table_grad[None], grad_in[None], grad_out[None])


def solution(mesh):
    in_specs = (
        P("table", None, None),
        P("table", None),
        P("table", "expert", None),
        P("table", "expert", None, None),
        P("table", "expert", None),
        P(),
        P(),
        P("expert", "table", None),
        P("table", None, "expert"),
        P("table", "expert", None),
        P(),
        P(),
        P("expert", "table", None),
    )
    out_specs = (
        P("expert", "table", None),
        P("table", "expert", None),
        P("table", None, "expert"),
        P("table", "expert", None),
    )
    return jax.shard_map(local, mesh=mesh, in_specs=in_specs, out_specs=out_specs, check_vma=False)
```
